32 devices in a mesh: row: 8 (over z, core), col: 4 (over y, x).
Axes of the slice: x: 2, y: 2, z: 4, core: 2. Of those that a mesh axis runs over, the one named last changes fastest.
Arguments:
- out_cotangent: bfloat16 [512, 8192], P('row', 'col'), may hold values from -1.75 to 1.75
- saved_input: bfloat16 [512, 8192], P('row', 'col'), may hold values from -6 to 6
- scan_output: bfloat16 [512, 16384], P('col', 'row'), may hold values from -6 to 6
- gate_input: bfloat16 [512, 16384], P('col', 'row'), may hold values from -8 to 8
- branch_grad: bfloat16 [512, 16384], P('col', 'row'), may hold values from -1.75 to 1.75
- out_weight: bfloat16 [16384, 8192], P('row', 'col'), may hold values from -0.046875 to 0.046875
- in_weight: bfloat16 [8192, 2, 16384], P('col', None, 'row'), may hold values from -0.0625 to 0.0625
Outputs:
- input_grad: bfloat16 [512, 8192], P('row', 'col')
- scan_grad: bfloat16 [512, 16384], P('col', 'row')
- in_weight_grad: float32 [8192, 2, 16384], P('col', None, 'row')
- out_weight_grad: float32 [16384, 8192], P('row', 'col')
The draws below stay inside these ranges and needn't reach their ends.
All inputs are finite; a program needn't handle non-finite values.
Results may differ from the reference program's by a relative error of at most 0.025.
Values may be sent and summed in bfloat16 or wider, within the bound.
No kernel may reach another device: no remote copies, remote signals or barrier semaphores. Data moves between devices by JAX's collectives and lax.ppermute only.
A program may use at most 192 MiB of HBM per device.

```python
import jax
import jax.numpy as jnp
from jax import lax

D = 8192
E = 16384
TOKENS = 512
N_ROW = 8
N_COL = 4


def raised(values, key, source, target, blocks, factor):
    owner, partner = [(jnp.arange(values.shape[position]) // (values.shape[position] // blocks)).reshape([-1 if axis == position else 1 for axis in range(values.ndim)]) for position in (source, target)]
    chosen = jax.random.permutation(key, blocks)[partner]
    strong = (owner == chosen) | (owner == (partner + blocks // 2) % blocks)
    return jnp.where(strong, factor * values, values)


def shard_levels(own_key, dims, split, smallest, top_value):
    loudness = 1.0
    for dim, shards_of in split:
        draws = jax.random.uniform(jax.random.fold_in(jax.random.fold_in(own_key, 6), dim), (shards_of,), jnp.float32, smallest / len(split), top_value / len(split))
        loudness = loudness * jnp.repeat(jnp.exp(draws), dims[dim] // shards_of).reshape((-1,) + (1,) * (len(dims) - 1 - dim))
    return loudness


def noise(own_key, extent, spread, reach, pieces=(), kind=jnp.bfloat16):
    entries = jax.random.normal(own_key, extent, jnp.float32) * spread
    if len(pieces) > 0:
        entries = shard_levels(own_key, extent, pieces, -0.22, 0.18) * entries
    return jnp.clip(entries, min=-reach, max=reach).astype(kind)


def noise_with(key, dims, spread, limit, shards, heavy, kind=jnp.bfloat16):
    values = spread * jax.random.normal(key, dims, jnp.float32)
    if shards:
        values = values * shard_levels(key, dims, shards, -0.22, 0.18)
    return jnp.clip(raised(values, jax.random.fold_in(key, 3), *heavy), -limit, limit).astype(kind)


def setup_inputs(seed: int = 0) -> dict:
    streams_of = jax.random.split(jax.random.key(seed), 8)
    out_cotangent = noise_with(streams_of[0], (TOKENS, D), (1.0 / TOKENS ** 0.25), 1.75, ((0, 8), (1, 4)), (1, 0, 8, 2.0))
    saved_input = noise(streams_of[1], (TOKENS, D), 1.0, 6.0, ((0, 8), (1, 4)))
    scan_output = noise(streams_of[2], (TOKENS, E), 1.0, 6.0, ((0, 4), (1, 8)))
    gate_input = noise(streams_of[3], (TOKENS, E), 1.5, 8.0, ((0, 4), (1, 8)))
    branch_grad = noise_with(streams_of[4], (TOKENS, E), (1.0 / TOKENS ** 0.25), 1.75, ((0, 4), (1, 8)), (1, 0, 8, 2.0))
    out_weight = noise(streams_of[5], (E, D), E ** -0.5, 0.046875, ((0, 8), (1, 4)))
    in_weight = noise(streams_of[6], (D, 2, E), D ** -0.5, 0.0625, ((0, 4), (2, 8)))
    return dict(out_cotangent=out_cotangent, saved_input=saved_input, scan_output=scan_output, gate_input=gate_input, branch_grad=branch_grad, out_weight=out_weight, in_weight=in_weight)


def reference(out_cotangent, saved_input, scan_output, gate_input, branch_grad, out_weight, in_weight):
    gate_value = gate_input.astype(jnp.float32)
    sigmoid_gate = jax.nn.sigmoid(gate_value)
    silu_gate = gate_value * sigmoid_gate
    scan_value = scan_output.astype(jnp.float32)
    gated = (scan_value * silu_gate).astype(jnp.bfloat16)
    width = D // N_COL
    gated_grad = jnp.zeros((TOKENS, E), jnp.float32)
    for block in range(N_COL):
        part_rows = out_cotangent[:, block * width:(block + 1) * width]
        part_weight = out_weight[:, block * width:(block + 1) * width]
        partial_sum = lax.dot_general(part_rows, part_weight, (((1,), (1,)), ((), ())), preferred_element_type=jnp.float32)
        gated_grad = gated_grad + partial_sum.astype(jnp.bfloat16).astype(jnp.float32)
    gate_grad = (gated_grad * scan_value * sigmoid_gate * (1.0 + gate_value * (1.0 - sigmoid_gate))).astype(jnp.bfloat16)
    scan_grad = (gated_grad * silu_gate).astype(jnp.bfloat16)
    branch_weight = in_weight[:, 0, :]
    gate_weight = in_weight[:, 1, :]
    channels = E // N_ROW
    input_sum = jnp.zeros((TOKENS, D), jnp.float32)
    for block in range(N_ROW):
        low = block * channels
        high = low + channels
        term = lax.dot_general(branch_grad[:, low:high], branch_weight[:, low:high], (((1,), (1,)), ((), ())), preferred_element_type=jnp.float32)
        term = term + lax.dot_general(gate_grad[:, low:high], gate_weight[:, low:high], (((1,), (1,)), ((), ())), preferred_element_type=jnp.float32)
        input_sum = input_sum + term.astype(jnp.bfloat16).astype(jnp.float32)
    input_grad = input_sum.astype(jnp.bfloat16)
    branch_part = lax.dot_general(saved_input, branch_grad, (((0,), (0,)), ((), ())), preferred_element_type=jnp.float32)
    gate_part = lax.dot_general(saved_input, gate_grad, (((0,), (0,)), ((), ())), preferred_element_type=jnp.float32)
    in_weight_grad = jnp.stack([branch_part, gate_part], axis=1)
    out_weight_grad = lax.dot_general(gated, out_cotangent, (((0,), (0,)), ((), ())), preferred_element_type=jnp.float32)
    return input_grad, scan_grad, in_weight_grad, out_weight_grad
```

```python
import functools

import jax
import jax.numpy as jnp
from jax import lax
from jax.experimental import pallas as pl
from jax.experimental.pallas import tpu as pltpu
from jax.sharding import PartitionSpec as P

BF16 = jnp.bfloat16
F32 = jnp.float32
MIB = 2**20
WEIGHT = 8
LANES = 128
PARTNERS = (1, 2, 3)
COLUMN, CORE, CHIP = 0, 1, 2


def run(body, where, args, in_specs, outs, out_specs, grid, scratch=(), flops=0, moved=0, vmem=16, aliases=None):
    return pl.pallas_call(
        body,
        out_shape=outs,
        grid_spec=pltpu.PrefetchScalarGridSpec(
            num_scalar_prefetch=1,
            grid=grid,
            in_specs=in_specs,
            out_specs=out_specs,
            scratch_shapes=list(scratch),
        ),
        input_output_aliases=aliases or {},
        cost_estimate=pl.CostEstimate(flops=flops, bytes_accessed=moved, transcendentals=0),
        compiler_params=pltpu.CompilerParams(vmem_limit_bytes=vmem * MIB),
    )(where, *args)


def far(pieces):
    return [pl.BlockSpec(memory_space=pl.ANY) for _ in pieces]


def lay(moves, sems, groups=1):
    first = pl.program_id(0) == 0
    copies = [pltpu.make_async_copy(piece, place, sems.at[index]) for index, (piece, place) in enumerate(moves)]
    size = len(copies) // groups

    @pl.when(first)
    def _():
        for copy in copies:
            copy.start()

    def arrived(group):
        @pl.when(first)
        def _():
            for copy in copies[group * size : (group + 1) * size]:
                copy.wait()

    return arrived


DEPTH = 3
PARTS = 4


def stream(source, buffer, sems):
    step, steps = pl.program_id(0), pl.num_programs(0)
    rows = buffer.shape[1] // PARTS

    def copies(step):
        slot = lax.rem(step, DEPTH)
        for part in range(PARTS):
            here = pl.ds(part * rows, rows)
            yield pltpu.make_async_copy(source(step).at[here], buffer.at[slot, here], sems.at[slot, part])

    @pl.when(step == 0)
    def _():
        for ahead in range(DEPTH - 1):
            for copy in copies(ahead):
                copy.start()

    @pl.when(step + DEPTH - 1 < steps)
    def _():
        for copy in copies(step + DEPTH - 1):
            copy.start()

    for copy in copies(step):
        copy.wait()
    return buffer.at[lax.rem(step, DEPTH)]


def streamed(shape, kind):
    return [pltpu.VMEM((DEPTH, *shape), kind), pltpu.SemaphoreType.DMA((DEPTH, PARTS))]


HBM = pl.BlockSpec(memory_space=pltpu.HBM)


def stay(value):
    return pltpu.with_memory_space_constraint(value, pltpu.HBM)


def at(start, size):
    return pl.ds(pl.multiple_of(start, size), size)


def dot_nt(rows, weight):
    return lax.dot_general(rows, weight, (((1,), (1,)), ((), ())), preferred_element_type=F32)


def dot_turned(rows, weight):
    return dot_nt(weight, rows).T


def dot_nn(rows, weight):
    return lax.dot_general(rows, weight, (((1,), (0,)), ((), ())), preferred_element_type=F32)


def split_body(where, source, branch, gate, order, *buffers):
    lines = buffers[0].shape[1]
    packed = stream(lambda step: source.at[at(step * lines, lines)], *buffers)

    @pl.when(pl.program_id(0) == 0)
    def _():
        row = lax.broadcasted_iota(jnp.int32, (256, 256), 0)
        column = lax.broadcasted_iota(jnp.int32, (256, 256), 1)
        source = (row & 7) * 32 + ((row >> 3) & 15) * 2 + (row >> 7)
        order[...] = jnp.where(column == source, 1.0, 0.0).astype(BF16)

    for group in range(branch.shape[0] // 16):
        low, high = (packed[pl.ds((2 * group + part) * 256, 256), :] for part in range(2))
        moved = dot_nn(order[...], jnp.concatenate([low, high], axis=1))
        parts = [moved[:, part * LANES : (part + 1) * LANES].reshape(2, 16, 1, 8, LANES) for part in range(2)]
        rows = jnp.concatenate(parts, axis=2).reshape(2, 16, 16, LANES).astype(BF16)
        for half, out in enumerate((branch, gate)):
            for tile in range(16):
                out[pl.ds(group * 16, 16), tile * LANES : (tile + 1) * LANES] = rows[half, tile]


def split_weight(where, in_weight):
    features, _, channels = in_weight.shape
    packed = (
        in_weight.reshape(features, 2, channels // LANES, LANES)
        .transpose(0, 2, 1, 3)
        .reshape(features * 2 * channels // LANES, LANES)
    )
    block = 128
    out = pltpu.HBM((features, channels), BF16)
    out_spec = pl.BlockSpec((block, channels), lambda i, *_: (i, 0))
    return run(
        split_body,
        where,
        (stay(packed),),
        [HBM],
        [out, out],
        [out_spec, out_spec],
        (features // block,),
        scratch=[pltpu.VMEM((256, 256), BF16), *streamed((block * 2 * channels // LANES, LANES), BF16)],
        flops=WEIGHT * 512 * 2 * features * channels,
        moved=WEIGHT * 8 * features * channels,
    )


def share_body(where, *refs):
    pieces, source, own, sends, rows, sems, buffers = refs[:4], refs[4], refs[5], refs[6:9], *refs[9:11], refs[11:]
    block = buffers[0].shape[1]
    weight = stream(lambda step: source.at[at(step * block, block)], *buffers)
    first = where[COLUMN] ^ where[CHIP]
    lay([(piece, rows.at[at((first ^ index) * 64, 64)]) for index, piece in enumerate(pieces)], sems)(0)

    total = dot_turned(rows[...], weight[...])
    own[...] = total[:64]
    for index, send in enumerate(sends):
        send[...] = total[(index + 1) * 64 : (index + 2) * 64].astype(BF16)


def share(where, pieces, weight):
    channels, features = weight.shape
    block = 512
    spec = pl.BlockSpec((64, block), lambda i, *_: (0, i))
    own, send = jax.ShapeDtypeStruct((64, channels), F32), pltpu.HBM((64, channels), BF16)
    return run(
        share_body,
        where,
        (*pieces, stay(weight)),
        far(pieces) + [HBM],
        [own, send, send, send],
        [spec] * 4,
        (channels // block,),
        scratch=[
            pltpu.VMEM((256, features), BF16),
            pltpu.SemaphoreType.DMA((4,)),
            *streamed((block, features), BF16),
        ],
        flops=2 * 256 * channels * features // WEIGHT,
        moved=2 * channels * features // WEIGHT,
    )


def gate_body(where, own, *refs):
    received, scan, gate = refs[:3], refs[3], refs[4]
    gate_grad, scan_grad = refs[-2:]
    summed = own[...]
    for term in received:
        summed = summed + term[...].astype(F32)
    value = gate[...].astype(F32)
    sigmoid = jax.nn.sigmoid(value)
    scan_value = scan[...].astype(F32)
    gate_grad[...] = (summed * scan_value * sigmoid * (1.0 + value * (1.0 - sigmoid))).astype(BF16)
    scan_grad[...] = (summed * (value * sigmoid)).astype(BF16)


def gate_step(where, own, received, scan, gate, previous):
    channels = scan.shape[1]
    block = 512
    spec = pl.BlockSpec((64, block), lambda i, *_: (0, i))
    mine = pl.BlockSpec((64, block), lambda i, where: (where[CORE], i))
    args = [own, *received, scan, gate]
    specs = [spec] * 4 + [mine, mine]
    aliases = {}
    if previous is not None:
        args.append(previous)
        specs.append(pl.BlockSpec(memory_space=pl.ANY))
        aliases = {7: 1}
    return run(
        gate_body,
        where,
        args,
        specs,
        [jax.ShapeDtypeStruct((64, channels), BF16), jax.ShapeDtypeStruct(scan.shape, BF16)],
        [spec, mine],
        (channels // block,),
        flops=WEIGHT * 64 * channels * 16,
        moved=WEIGHT * 64 * channels * 16,
        aliases=aliases,
    )


def branch_body(where, *refs):
    branch, source, mine, other, rows, sems, *buffers = refs
    block = buffers[0].shape[1]
    weight = stream(lambda step: source.at[at(step * block, block)], *buffers)
    core = where[CORE]
    moves = []
    for index in range(4):
        start = (where[CHIP] ^ index) * 128
        moves.append((branch.at[at(start + core * 64, 64)], rows.at[pl.ds(index * 64, 64)]))
        moves.append((branch.at[at(start + (1 - core) * 64, 64)], rows.at[pl.ds(256 + index * 64, 64)]))
    lay(moves, sems)(0)
    total = dot_nt(rows[...], weight[...])
    mine[...] = total[:256].reshape(mine.shape)
    other[...] = total[256:].reshape(other.shape).astype(BF16)


def branch_part(where, branch, weight):
    features, channels = weight.shape
    block = 512
    spec = pl.BlockSpec((4, 64, block), lambda i, *_: (0, 0, i))
    return run(
        branch_body,
        where,
        (branch, stay(weight)),
        [pl.BlockSpec(memory_space=pl.ANY), HBM],
        [pltpu.HBM((4, 64, features), F32), pltpu.HBM((4, 64, features), BF16)],
        [spec, spec],
        (features // block,),
        scratch=[
            pltpu.VMEM((512, channels), BF16),
            pltpu.SemaphoreType.DMA((8,)),
            *streamed((block, channels), BF16),
        ],
        flops=2 * 512 * channels * features // WEIGHT,
        moved=2 * channels * features // WEIGHT,
    )


def input_body(where, *refs):
    pieces, source, branch, out, rows, sems, buffers = refs[:4], *refs[4:9], refs[9:]
    block = buffers[0].shape[1]
    weight = stream(lambda step: source.at[at(step * block, block)], *buffers)
    first = where[COLUMN] ^ where[CHIP]
    lay([(piece, rows.at[at((first ^ index) * 64, 64)]) for index, piece in enumerate(pieces)], sems)(0)
    total = dot_turned(rows[...], weight[...])
    out[...] = (total.reshape(out.shape) + branch[...].astype(F32)).astype(out.dtype)


def input_part(where, pieces, weight, branch):
    features, channels = weight.shape
    block = 512
    spec = pl.BlockSpec((4, 64, block), lambda i, *_: (0, 0, i))
    return run(
        input_body,
        where,
        (*pieces, stay(weight), stay(branch)),
        far(pieces) + [HBM, spec],
        jax.ShapeDtypeStruct((4, 64, features), branch.dtype),
        spec,
        (features // block,),
        scratch=[
            pltpu.VMEM((256, channels), BF16),
            pltpu.SemaphoreType.DMA((4,)),
            *streamed((block, channels), BF16),
        ],
        flops=WEIGHT * 2 * 256 * channels * features,
        moved=WEIGHT * 2 * channels * features,
    )


def combine_body(where, here, there, *outs):
    for index, out in enumerate(outs):
        out[...] = (here[index] + there[index].astype(F32)).astype(out.dtype)


def combine(where, here, there):
    features = here.shape[2]
    block = 512
    four = pl.BlockSpec((4, 64, block), lambda i, *_: (0, 0, i))
    one = pl.BlockSpec((64, block), lambda i, *_: (0, i))
    return run(
        combine_body,
        where,
        (here, there),
        [four, four],
        [pltpu.HBM((64, features), F32)] + [jax.ShapeDtypeStruct((64, features), BF16)] * 3,
        [one] * 4,
        (features // block,),
        flops=256 * features,
        moved=256 * features * 9,
    )


def in_grad_body(block, tiles, where, *refs):
    branch, mine, other, saved, out, rows, order, held, sems, out_sems = refs[0], refs[1:5], refs[5:9], *refs[9:]
    step, steps = pl.program_id(0), pl.num_programs(0)
    slot = lax.rem(step, 2)
    group, lines = block // 8, 2 * tiles
    pitch = group * lines + 1
    moves = [(branch.at[pl.ds(start, 64)], rows.at[0, pl.ds(start, 64)]) for start in range(0, 512, 64)]
    for index in range(4):
        start = (where[COLUMN] ^ index) * 128
        moves.append((mine[index], rows.at[1, at(start + where[CORE] * 64, 64)]))
        moves.append((other[index], rows.at[1, at(start + (1 - where[CORE]) * 64, 64)]))
    arrived = lay(moves, sems, 2)

    @pl.when(step == 0)
    def _():
        row = lax.broadcasted_iota(jnp.int32, (block, block), 0)
        column = lax.broadcasted_iota(jnp.int32, (block, block), 1)
        order[...] = jnp.where(column == (row & 7) * group + (row >> 3), 1.0, 0.0).astype(BF16)

    def copy(step, slot, part):
        return pltpu.make_async_copy(
            held.at[slot, pl.ds(part * pitch, group * lines)],
            out.at[pl.ds(pl.multiple_of((step * 8 + part) * group * lines, 8), group * lines)],
            out_sems.at[slot, part],
        )

    @pl.when(step >= 2)
    def _():
        for part in range(8):
            copy(step - 2, slot, part).wait()

    left = dot_nt(order[...], saved[...]).astype(BF16)
    width = 256
    for half in range(2):
        arrived(half)
        for first in range(0, tiles * LANES, width):
            total = dot_nn(left, rows[half, :, first : first + width])
            for tile in range(width // LANES):
                line = 2 * (first // LANES + tile) + half
                for index in range(group):
                    held[slot, pl.ds(index * lines + line, 8, stride=pitch), :] = total[
                        index * 8 : (index + 1) * 8, tile * LANES : (tile + 1) * LANES
                    ]
    for part in range(8):
        copy(step, slot, part).start()

    @pl.when(step == steps - 1)
    def _():
        for part in range(8):
            copy(step - 1, 1 - slot, part).wait()
        for part in range(8):
            copy(step, slot, part).wait()


def in_grad(where, branch, mine, other, saved):
    tokens, features = saved.shape
    channels = mine[0].shape[1]
    tiles = channels // LANES
    block = 256
    pieces = (branch, *mine, *other)
    held = -(-(block * 2 * tiles + 8) // 8) * 8
    out = run(
        functools.partial(in_grad_body, block, tiles),
        where,
        (*map(stay, pieces), stay(saved)),
        far(pieces) + [pl.BlockSpec((tokens, block), lambda i, *_: (0, i))],
        jax.ShapeDtypeStruct((features * 2 * tiles, LANES), F32),
        pl.BlockSpec(memory_space=pl.ANY),
        (features // block,),
        scratch=[
            pltpu.VMEM((2, tokens, channels), BF16),
            pltpu.VMEM((block, block), BF16),
            pltpu.VMEM((2, held, LANES), F32),
            pltpu.SemaphoreType.DMA((16,)),
            pltpu.SemaphoreType.DMA((2, 8)),
        ],
        flops=4 * tokens * features * channels,
        moved=8 * features * channels + 2 * tokens * (features + 2 * channels),
        vmem=32,
    )
    return out.reshape(features, tiles, 2, LANES).transpose(0, 2, 1, 3).reshape(features, 2, channels)


def out_grad_body(where, *refs):
    mine, other, gated, out, right, same, held, sems, out_sems = refs[:4], refs[4:8], *refs[8:]
    step, steps = pl.program_id(0), pl.num_programs(0)
    slot = lax.rem(step, 2)
    _, columns, block, width = held.shape
    moves = []
    for index in range(4):
        start = (where[CHIP] ^ index) * 128
        moves.append((mine[index], right.at[at(start + where[CORE] * 64, 64)]))
        moves.append((other[index], right.at[at(start + (1 - where[CORE]) * 64, 64)]))
    arrived = lay(moves, sems)

    @pl.when(step == 0)
    def _():
        row = lax.broadcasted_iota(jnp.int32, (block, block), 0)
        column = lax.broadcasted_iota(jnp.int32, (block, block), 1)
        same[...] = jnp.where(row == column, 1.0, 0.0).astype(BF16)

    def copy(step, slot, part):
        return pltpu.make_async_copy(
            held.at[slot, part],
            out.at[at(step * block, block), pl.ds(part * width, width)],
            out_sems.at[slot, part],
        )

    rows = dot_nt(same[...], gated[...]).astype(BF16)
    arrived(0)
    for part in range(columns):

        @pl.when(step >= 2)
        def _():
            copy(step - 2, slot, part).wait()

        held[slot, part] = dot_nn(rows, right[:, part * width : (part + 1) * width])
        copy(step, slot, part).start()

    @pl.when(step == steps - 1)
    def _():
        for part in range(columns):
            copy(step - 1, 1 - slot, part).wait()
        for part in range(columns):
            copy(step, slot, part).wait()


def out_grad(where, gated, mine, other):
    tokens, channels = gated.shape
    features = mine[0].shape[1]
    block, width = 512, 512
    pieces = (*mine, *other)
    return run(
        out_grad_body,
        where,
        tuple(map(stay, (*pieces, gated))),
        far(pieces) + [pl.BlockSpec((tokens, block), lambda i, *_: (0, i))],
        jax.ShapeDtypeStruct((channels, features), F32),
        pl.BlockSpec(memory_space=pl.ANY),
        (channels // block,),
        scratch=[
            pltpu.VMEM((tokens, features), BF16),
            pltpu.VMEM((block, block), BF16),
            pltpu.VMEM((2, features // width, block, width), F32),
            pltpu.SemaphoreType.DMA((8,)),
            pltpu.SemaphoreType.DMA((2, features // width)),
        ],
        flops=2 * tokens * channels * features,
        moved=4 * channels * features + 2 * tokens * (channels + features),
        vmem=24,
    )


def to_plane(value, partner):
    return lax.ppermute(value, "col", [(index, index ^ partner) for index in range(4)])


def to_chip(value, partner):
    return lax.ppermute(value, "row", [(index, index ^ (2 * partner)) for index in range(8)])


def to_other_core(value):
    return lax.ppermute(value, "row", [(index, index ^ 1) for index in range(8)])


def after(value, *earlier):
    return lax.optimization_barrier((value, *earlier))[0]


def plane_per_device(
    out_cotangent, saved_input, scan_output, gate_input, branch_grad, out_weight, in_weight
):
    column, row = lax.axis_index("col"), lax.axis_index("row")
    core, chip = row % 2, row // 2
    mine = jnp.stack([column, core, chip]).astype(jnp.int32)
    other = jnp.stack([column, 1 - core, chip]).astype(jnp.int32)

    beside = to_other_core(out_cotangent)
    branch = lax.all_gather(branch_grad, "col", axis=0, tiled=True)
    gate_value = gate_input.astype(F32)
    gated = (scan_output.astype(F32) * (gate_value * jax.nn.sigmoid(gate_value))).astype(BF16)
    branch_weight, gate_weight = split_weight(mine, after(in_weight, beside, gated))
    cot_other = (beside, *(to_chip(beside, partner) for partner in PARTNERS))
    cot_mine = (out_cotangent, *(to_other_core(after(block, branch_weight)) for block in cot_other[1:]))

    share_other = share(other, cot_other, after(out_weight, branch_weight))
    share_mine = share(mine, after(cot_mine, share_other[0]), out_weight)
    saved = lax.all_gather(after(saved_input, share_other[0]), "row", axis=0, tiled=True)
    sums_other = [to_plane(send, partner) for send, partner in zip(share_other[1:], PARTNERS)]
    sums_mine = [to_plane(send, partner) for send, partner in zip(share_mine[1:], PARTNERS)]
    own = after(share_other[0], share_mine[0], branch)
    grad_other, scan_grad = gate_step(other, own, sums_other, scan_output, gate_input, None)
    grad_other = (grad_other, *(to_plane(grad_other, partner) for partner in PARTNERS))
    branch_mine, branch_other = branch_part(mine, after(branch, grad_other[0], sums_mine[0]), branch_weight)
    own = after(share_mine[0], branch_mine)
    grad_mine, scan_grad = gate_step(mine, own, sums_mine, scan_output, gate_input, scan_grad)
    grad_mine = (grad_mine, *(to_plane(grad_mine, partner) for partner in PARTNERS))

    there = input_part(other, grad_other, after(gate_weight, saved), branch_other)
    here = input_part(mine, grad_mine, gate_weight, branch_mine)
    total, *sends = combine(mine, here, to_other_core(there))
    terms = [to_chip(send, partner) for send, partner in zip(sends, PARTNERS)]

    gated = lax.all_gather(after(gated, there), "col", axis=0, tiled=True)
    in_weight_grad = in_grad(mine, branch, grad_mine, grad_other, after(saved, total))
    in_weight_grad, total = lax.optimization_barrier((in_weight_grad, total))
    out_weight_grad = out_grad(mine, gated, after(cot_mine, total), cot_other)
    for term in terms:
        total = total + term.astype(F32)
    return (total.astype(BF16), scan_grad, in_weight_grad, out_weight_grad)


def gate_backward(summed, scan_output, gate_input):
    gate_value = gate_input.astype(jnp.float32)
    sigmoid_gate = jax.nn.sigmoid(gate_value)
    silu_gate = gate_value * sigmoid_gate
    scan_value = scan_output.astype(jnp.float32)
    gated = (scan_value * silu_gate).astype(jnp.bfloat16)
    gate_grad = (
        summed * scan_value * sigmoid_gate * (1.0 + gate_value * (1.0 - sigmoid_gate))
    ).astype(jnp.bfloat16)
    scan_grad = (summed * silu_gate).astype(jnp.bfloat16)
    return (gated, gate_grad, scan_grad)


def per_device(
    out_cotangent, saved_input, scan_output, gate_input, branch_grad, out_weight, in_weight
):
    cotangent = lax.all_gather(out_cotangent, "row", axis=0, tiled=True)
    shares = lax.psum_scatter(
        lax.dot_general(
            cotangent, out_weight, (((1,), (1,)), ((), ())), preferred_element_type=jnp.float32
        ).astype(jnp.bfloat16),
        "col",
        scatter_dimension=0,
        tiled=True,
    ).astype(jnp.float32)
    gated, gate_grad, scan_grad = gate_backward(shares, scan_output, gate_input)
    gated_all, branch_all, gate_grad_all = (
        lax.all_gather(gated, "col", axis=0, tiled=True),
        lax.all_gather(branch_grad, "col", axis=0, tiled=True),
        lax.all_gather(gate_grad, "col", axis=0, tiled=True),
    )
    out_weight_grad = lax.dot_general(
        gated_all, cotangent, (((0,), (0,)), ((), ())), preferred_element_type=jnp.float32
    )
    total = lax.dot_general(
        branch_all, in_weight[:, 0, :], (((1,), (1,)), ((), ())), preferred_element_type=jnp.float32
    ) + lax.dot_general(
        gate_grad_all, in_weight[:, 1, :], (((1,), (1,)), ((), ())), preferred_element_type=jnp.float32
    )
    input_grad = lax.psum_scatter(
        total.astype(jnp.bfloat16), "row", scatter_dimension=0, tiled=True
    )
    piece = lax.all_gather(saved_input, "row", axis=0, tiled=True)
    in_weight_grad = jnp.stack(
        [
            lax.dot_general(piece, grad, (((0,), (0,)), ((), ())), preferred_element_type=jnp.float32)
            for grad in (branch_all, gate_grad_all)
        ],
        axis=1,
    )
    return (input_grad, scan_grad, in_weight_grad, out_weight_grad)


def solution(mesh):
    rows, columns = mesh.shape["row"], mesh.shape["col"]
    body = plane_per_device if (rows, columns) == (8, 4) else per_device
    return jax.shard_map(
        body,
        mesh=mesh,
        in_specs=(
            P("row", "col"),
            P("row", "col"),
            P("col", "row"),
            P("col", "row"),
            P("col", "row"),
            P("row", "col"),
            P("col", None, "row"),
        ),
        out_specs=(P("row", "col"), P("col", "row"), P("col", None, "row"), P("row", "col")),
        check_vma=False,
    )
```

```python
import functools

import jax
import jax.numpy as jnp
from jax import lax
from jax.experimental import pallas as pl
from jax.experimental.pallas import tpu as pltpu
from jax.sharding import PartitionSpec as P

BF16 = jnp.bfloat16
F32 = jnp.float32
MIB = 2**20
WEIGHT = 8
LANES = 128
PARTNERS = (1, 2, 3)
COLUMN, CORE, CHIP = 0, 1, 2


def run(body, where, args, in_specs, outs, out_specs, grid, scratch=(), flops=0, moved=0, vmem=16, aliases=None):
    return pl.pallas_call(
        body,
        out_shape=outs,
        grid_spec=pltpu.PrefetchScalarGridSpec(
            num_scalar_prefetch=1,
            grid=grid,
            in_specs=in_specs,
            out_specs=out_specs,
            scratch_shapes=list(scratch),
        ),
        input_output_aliases=aliases or {},
        cost_estimate=pl.CostEstimate(flops=flops, bytes_accessed=moved, transcendentals=0),
        compiler_params=pltpu.CompilerParams(vmem_limit_bytes=vmem * MIB),
    )(where, *args)


def far(pieces):
    return [pl.BlockSpec(memory_space=pl.ANY) for _ in pieces]


def lay(moves, sems):
    @pl.when(pl.program_id(0) == 0)
    def _():
        copies = [pltpu.make_async_copy(piece, place, sems.at[index]) for index, (piece, place) in enumerate(moves)]
        for copy in copies:
            copy.start()
        for copy in copies:
            copy.wait()


DEPTH = 3
PARTS = 4


def stream(source, buffer, sems):
    step, steps = pl.program_id(0), pl.num_programs(0)
    rows = buffer.shape[1] // PARTS

    def copies(step):
        slot = lax.rem(step, DEPTH)
        for part in range(PARTS):
            here = pl.ds(part * rows, rows)
            yield pltpu.make_async_copy(source(step).at[here], buffer.at[slot, here], sems.at[slot, part])

    @pl.when(step == 0)
    def _():
        for ahead in range(DEPTH - 1):
            for copy in copies(ahead):
                copy.start()

    @pl.when(step + DEPTH - 1 < steps)
    def _():
        for copy in copies(step + DEPTH - 1):
            copy.start()

    for copy in copies(step):
        copy.wait()
    return buffer.at[lax.rem(step, DEPTH)]


def streamed(shape, kind):
    return [pltpu.VMEM((DEPTH, *shape), kind), pltpu.SemaphoreType.DMA((DEPTH, PARTS))]


HBM = pl.BlockSpec(memory_space=pltpu.HBM)


def stay(value):
    return pltpu.with_memory_space_constraint(value, pltpu.HBM)


def at(start, size):
    return pl.ds(pl.multiple_of(start, size), size)


def dot_nt(rows, weight):
    return lax.dot_general(rows, weight, (((1,), (1,)), ((), ())), preferred_element_type=F32)


def dot_turned(rows, weight):
    return dot_nt(weight, rows).T


def dot_nn(rows, weight):
    return lax.dot_general(rows, weight, (((1,), (0,)), ((), ())), preferred_element_type=F32)


def split_body(where, source, branch, gate, order, *buffers):
    lines = buffers[0].shape[1]
    packed = stream(lambda step: source.at[at(step * lines, lines)], *buffers)

    @pl.when(pl.program_id(0) == 0)
    def _():
        row = lax.broadcasted_iota(jnp.int32, (256, 256), 0)
        column = lax.broadcasted_iota(jnp.int32, (256, 256), 1)
        source = (row & 7) * 32 + ((row >> 3) & 15) * 2 + (row >> 7)
        order[...] = jnp.where(column == source, 1.0, 0.0).astype(BF16)

    for group in range(branch.shape[0] // 16):
        low, high = (packed[pl.ds((2 * group + part) * 256, 256), :] for part in range(2))
        moved = dot_nn(order[...], jnp.concatenate([low, high], axis=1))
        parts = [moved[:, part * LANES : (part + 1) * LANES].reshape(2, 16, 1, 8, LANES) for part in range(2)]
        rows = jnp.concatenate(parts, axis=2).reshape(2, 16, 16, LANES).astype(BF16)
        for half, out in enumerate((branch, gate)):
            for tile in range(16):
                out[pl.ds(group * 16, 16), tile * LANES : (tile + 1) * LANES] = rows[half, tile]


def split_weight(where, in_weight):
    features, _, channels = in_weight.shape
    packed = (
        in_weight.reshape(features, 2, channels // LANES, LANES)
        .transpose(0, 2, 1, 3)
        .reshape(features * 2 * channels // LANES, LANES)
    )
    block = 128
    out = pltpu.HBM((features, channels), BF16)
    out_spec = pl.BlockSpec((block, channels), lambda i, *_: (i, 0))
    return run(
        split_body,
        where,
        (stay(packed),),
        [HBM],
        [out, out],
        [out_spec, out_spec],
        (features // block,),
        scratch=[pltpu.VMEM((256, 256), BF16), *streamed((block * 2 * channels // LANES, LANES), BF16)],
        flops=WEIGHT * 512 * 2 * features * channels,
        moved=WEIGHT * 8 * features * channels,
    )


def share_body(where, *refs):
    pieces, rest, source, own, sends, rows, sems, buffers = refs[:4], *refs[4:7], refs[7:10], *refs[10:12], refs[12:]
    block = buffers[0].shape[1]
    weight = stream(lambda step: source.at[at(step * block, block)], *buffers)
    first = where[COLUMN] ^ where[CHIP]
    near = pieces[0].shape[1]
    far_columns = pl.ds(near, rest.shape[1])
    moves = []
    for index, piece in enumerate(pieces):
        moves.append((piece, rows.at[at((first ^ index) * 64, 64), pl.ds(0, near)]))
        here = at((where[COLUMN] ^ index) * 128 + where[CORE] * 64, 64)
        moves.append((rest.at[here], rows.at[pl.ds(index * 64, 64), far_columns]))
    lay(moves, sems)

    total = dot_turned(rows[...], weight[...])
    own[...] = total[:64]
    for index, send in enumerate(sends):
        send[...] = total[(index + 1) * 64 : (index + 2) * 64].astype(BF16)


def share(where, pieces, rest, weight, own, send):
    channels, features = weight.shape
    block = 512
    spec = pl.BlockSpec((64, block), lambda i, *_: (0, i))
    return run(
        share_body,
        where,
        (*pieces, stay(rest), stay(weight)),
        far(pieces) + [HBM, HBM],
        [own((64, channels), F32)] + [send((64, channels), BF16)] * 3,
        [spec] * 4,
        (channels // block,),
        scratch=[
            pltpu.VMEM((256, features), BF16),
            pltpu.SemaphoreType.DMA((8,)),
            *streamed((block, features), BF16),
        ],
        flops=2 * 256 * channels * features // WEIGHT,
        moved=2 * channels * features // WEIGHT,
    )


def gate_body(where, own, *refs):
    received, scan, gate = refs[:3], refs[3], refs[4]
    gate_grad, scan_grad = refs[-2:]
    summed = own[...]
    for term in received:
        summed = summed + term[...].astype(F32)
    value = gate[...].astype(F32)
    sigmoid = jax.nn.sigmoid(value)
    scan_value = scan[...].astype(F32)
    gate_grad[...] = (summed * scan_value * sigmoid * (1.0 + value * (1.0 - sigmoid))).astype(BF16)
    scan_grad[...] = (summed * (value * sigmoid)).astype(BF16)


def gate_step(where, own, received, scan, gate, previous):
    channels = scan.shape[1]
    block = channels
    spec = pl.BlockSpec((64, block), lambda i, *_: (0, i))
    mine = pl.BlockSpec((64, block), lambda i, where: (where[CORE], i))
    args = [own, *received, scan, gate]
    specs = [spec] * 4 + [mine, mine]
    aliases = {}
    if previous is not None:
        args.append(previous)
        specs.append(pl.BlockSpec(memory_space=pl.ANY))
        aliases = {7: 1}
    return run(
        gate_body,
        where,
        args,
        specs,
        [jax.ShapeDtypeStruct((64, channels), BF16), jax.ShapeDtypeStruct(scan.shape, BF16)],
        [spec, mine],
        (channels // block,),
        flops=WEIGHT * 64 * channels * 16,
        moved=WEIGHT * 64 * channels * 16,
        aliases=aliases,
    )


def branch_body(where, *refs):
    branch, source, mine, other, rows, sems, *buffers = refs
    block = buffers[0].shape[1]
    weight = stream(lambda step: source.at[at(step * block, block)], *buffers)
    core = where[CORE]
    moves = []
    for index in range(4):
        start = (where[CHIP] ^ index) * 128
        moves.append((branch.at[at(start + core * 64, 64)], rows.at[pl.ds(index * 64, 64)]))
        moves.append((branch.at[at(start + (1 - core) * 64, 64)], rows.at[pl.ds(256 + index * 64, 64)]))
    lay(moves, sems)
    total = dot_nt(rows[...], weight[...])
    mine[...] = total[:256].reshape(mine.shape)
    other[...] = total[256:].reshape(other.shape).astype(BF16)


def branch_part(where, branch, weight):
    features, channels = weight.shape
    block = 512
    spec = pl.BlockSpec((4, 64, block), lambda i, *_: (0, 0, i))
    return run(
        branch_body,
        where,
        (branch, stay(weight)),
        [pl.BlockSpec(memory_space=pl.ANY), HBM],
        [pltpu.HBM((4, 64, features), F32), pltpu.HBM((4, 64, features), BF16)],
        [spec, spec],
        (features // block,),
        scratch=[
            pltpu.VMEM((512, channels), BF16),
            pltpu.SemaphoreType.DMA((8,)),
            *streamed((block, channels), BF16),
        ],
        flops=2 * 512 * channels * features // WEIGHT,
        moved=2 * channels * features // WEIGHT,
    )


def input_body(where, *refs):
    pieces, source, branch, out, rows, sems, buffers = refs[:4], *refs[4:9], refs[9:]
    block = buffers[0].shape[1]
    weight = stream(lambda step: source.at[at(step * block, block)], *buffers)
    first = where[COLUMN] ^ where[CHIP]
    lay([(piece, rows.at[at((first ^ index) * 64, 64)]) for index, piece in enumerate(pieces)], sems)
    total = dot_turned(rows[...], weight[...])
    out[...] = (total.reshape(out.shape) + branch[...].astype(F32)).astype(out.dtype)


def input_part(where, pieces, weight, branch):
    features, channels = weight.shape
    block = 512
    spec = pl.BlockSpec((4, 64, block), lambda i, *_: (0, 0, i))
    return run(
        input_body,
        where,
        (*pieces, stay(weight), stay(branch)),
        far(pieces) + [HBM, spec],
        jax.ShapeDtypeStruct((4, 64, features), branch.dtype),
        spec,
        (features // block,),
        scratch=[
            pltpu.VMEM((256, channels), BF16),
            pltpu.SemaphoreType.DMA((4,)),
            *streamed((block, channels), BF16),
        ],
        flops=WEIGHT * 2 * 256 * channels * features,
        moved=WEIGHT * 2 * channels * features,
    )


def combine_body(where, here, there, *outs):
    for index, out in enumerate(outs):
        out[...] = (here[index] + there[index].astype(F32)).astype(out.dtype)


def combine(where, here, there):
    features = here.shape[2]
    block = features
    four = pl.BlockSpec((4, 64, block), lambda i, *_: (0, 0, i))
    one = pl.BlockSpec((64, block), lambda i, *_: (0, i))
    return run(
        combine_body,
        where,
        (here, there),
        [four, four],
        [pltpu.HBM((64, features), F32)] + [jax.ShapeDtypeStruct((64, features), BF16)] * 3,
        [one] * 4,
        (features // block,),
        flops=256 * features,
        moved=256 * features * 9,
    )


def in_grad_body(block, tiles, where, *refs):
    branch, mine, other, saved, out, rows, order, held, sems, out_sems = refs[0], refs[1:5], refs[5:9], *refs[9:]
    step, steps = pl.program_id(0), pl.num_programs(0)
    slot = lax.rem(step, 2)
    group, lines = block // 8, 2 * tiles
    pitch = group * lines + 1
    moves = [(branch.at[pl.ds(start, 128)], rows.at[0, pl.ds(start, 128)]) for start in range(0, 512, 128)]
    for index in range(4):
        start = (where[COLUMN] ^ index) * 128
        moves.append((mine[index], rows.at[1, at(start + where[CORE] * 64, 64)]))
        moves.append((other[index], rows.at[1, at(start + (1 - where[CORE]) * 64, 64)]))
    lay(moves, sems)

    @pl.when(step == 0)
    def _():
        row = lax.broadcasted_iota(jnp.int32, (block, block), 0)
        column = lax.broadcasted_iota(jnp.int32, (block, block), 1)
        order[...] = jnp.where(column == (row & 7) * group + (row >> 3), 1.0, 0.0).astype(BF16)

    def copy(step, slot, part):
        return pltpu.make_async_copy(
            held.at[slot, pl.ds(part * pitch, group * lines)],
            out.at[pl.ds(pl.multiple_of((step * 8 + part) * group * lines, 8), group * lines)],
            out_sems.at[slot, part],
        )

    @pl.when(step >= 2)
    def _():
        for part in range(8):
            copy(step - 2, slot, part).wait()

    left = dot_nt(order[...], saved[...]).astype(BF16)
    width = 256
    for half in range(2):
        for first in range(0, tiles * LANES, width):
            total = dot_nn(left, rows[half, :, first : first + width])
            for tile in range(width // LANES):
                line = 2 * (first // LANES + tile) + half
                for index in range(group):
                    held[slot, pl.ds(index * lines + line, 8, stride=pitch), :] = total[
                        index * 8 : (index + 1) * 8, tile * LANES : (tile + 1) * LANES
                    ]
    for part in range(8):
        copy(step, slot, part).start()

    @pl.when(step == steps - 1)
    def _():
        for part in range(8):
            copy(step - 1, 1 - slot, part).wait()
        for part in range(8):
            copy(step, slot, part).wait()


def in_grad(where, branch, mine, other, saved):
    tokens, features = saved.shape
    channels = mine[0].shape[1]
    tiles = channels // LANES
    block = 256
    pieces = (branch, *mine, *other)
    held = -(-(block * 2 * tiles + 8) // 8) * 8
    out = run(
        functools.partial(in_grad_body, block, tiles),
        where,
        (*map(stay, pieces), stay(saved)),
        far(pieces) + [pl.BlockSpec((tokens, block), lambda i, *_: (0, i))],
        jax.ShapeDtypeStruct((features * 2 * tiles, LANES), F32),
        pl.BlockSpec(memory_space=pl.ANY),
        (features // block,),
        scratch=[
            pltpu.VMEM((2, tokens, channels), BF16),
            pltpu.VMEM((block, block), BF16),
            pltpu.VMEM((2, held, LANES), F32),
            pltpu.SemaphoreType.DMA((12,)),
            pltpu.SemaphoreType.DMA((2, 8)),
        ],
        flops=4 * tokens * features * channels,
        moved=8 * features * channels + 2 * tokens * (features + 2 * channels),
        vmem=32,
    )
    return out.reshape(features, tiles, 2, LANES).transpose(0, 2, 1, 3).reshape(features, 2, channels)


def out_grad_body(where, *refs):
    mine, other, rest, gated, out, right, same, sems = refs[:4], refs[4:8], *refs[8:]
    block = same.shape[0]
    near = pl.ds(0, mine[0].shape[1])
    moves = [(rest, right.at[:, pl.ds(mine[0].shape[1], rest.shape[1])])]
    for index in range(4):
        start = (where[CHIP] ^ index) * 128
        moves.append((mine[index], right.at[at(start + where[CORE] * 64, 64), near]))
        moves.append((other[index], right.at[at(start + (1 - where[CORE]) * 64, 64), near]))
    lay(moves, sems)

    @pl.when(pl.program_id(0) == 0)
    def _():
        row = lax.broadcasted_iota(jnp.int32, (block, block), 0)
        column = lax.broadcasted_iota(jnp.int32, (block, block), 1)
        same[...] = jnp.where(row == column, 1.0, 0.0).astype(BF16)

    rows = dot_nt(same[...], gated[...]).astype(BF16)
    width = 512
    for first in range(0, out.shape[1], width):
        here = slice(first, first + width)
        out[:, here] = dot_nn(rows, right[:, here])


def out_grad(where, gated, mine, other, rest):
    tokens, channels = gated.shape
    features = mine[0].shape[1] + rest.shape[1]
    block = 512
    pieces = (*mine, *other)
    return run(
        out_grad_body,
        where,
        tuple(map(stay, (*pieces, rest, gated))),
        far(pieces) + [HBM, pl.BlockSpec((tokens, block), lambda i, *_: (0, i))],
        jax.ShapeDtypeStruct((channels, features), F32),
        pl.BlockSpec((block, features), lambda i, *_: (i, 0)),
        (channels // block,),
        scratch=[
            pltpu.VMEM((tokens, features), BF16),
            pltpu.VMEM((block, block), BF16),
            pltpu.SemaphoreType.DMA((9,)),
        ],
        flops=2 * tokens * channels * features,
        moved=4 * channels * features + 2 * tokens * (channels + features),
        vmem=24,
    )


def to_plane(value, partner):
    return lax.ppermute(value, "col", [(index, index ^ partner) for index in range(4)])


def to_chip(value, partner):
    return lax.ppermute(value, "row", [(index, index ^ (2 * partner)) for index in range(8)])


def to_other_core(value):
    return lax.ppermute(value, "row", [(index, index ^ 1) for index in range(8)])


def after(value, *earlier):
    return lax.optimization_barrier((value, *earlier))[0]


def plane_per_device(
    out_cotangent, saved_input, scan_output, gate_input, branch_grad, out_weight, in_weight
):
    column, row = lax.axis_index("col"), lax.axis_index("row")
    core, chip = row % 2, row // 2
    mine = jnp.stack([column, core, chip]).astype(jnp.int32)
    other = jnp.stack([column, 1 - core, chip]).astype(jnp.int32)

    near = out_cotangent.shape[1] * 3 // 4
    rest = lax.all_gather(out_cotangent[:, near:], "row", axis=0, tiled=True)
    own_near = out_cotangent[:, :near]
    beside = to_other_core(own_near)
    branch = lax.all_gather(after(branch_grad, beside), "col", axis=0, tiled=True)
    gate_value = gate_input.astype(F32)
    gated = (scan_output.astype(F32) * (gate_value * jax.nn.sigmoid(gate_value))).astype(BF16)
    branch_weight, gate_weight = split_weight(mine, after(in_weight, beside, gated))
    cot_other = (beside, *(to_chip(beside, partner) for partner in PARTNERS))
    cot_mine = (own_near, *(to_other_core(after(block, branch_weight)) for block in cot_other[1:]))

    share_other = share(other, cot_other, rest, after(out_weight, branch_weight), jax.ShapeDtypeStruct, pltpu.HBM)
    share_mine = share(mine, after(cot_mine, share_other[0]), rest, out_weight, pltpu.HBM, jax.ShapeDtypeStruct)
    saved = lax.all_gather(after(saved_input, share_other[0]), "row", axis=0, tiled=True)
    sums_other = [to_plane(send, partner) for send, partner in zip(share_other[1:], PARTNERS)]
    sums_mine = [to_plane(send, partner) for send, partner in zip(share_mine[1:], PARTNERS)]
    own = after(share_other[0], share_mine[0], branch)
    grad_other, scan_grad = gate_step(other, own, sums_other, scan_output, gate_input, None)
    grad_other = (grad_other, *(to_plane(grad_other, partner) for partner in PARTNERS))
    branch_mine, branch_other = branch_part(mine, after(branch, grad_other[0], sums_mine[0]), branch_weight)
    own = after(share_mine[0], branch_mine)
    grad_mine, scan_grad = gate_step(mine, own, sums_mine, scan_output, gate_input, scan_grad)
    grad_mine = (grad_mine, *(to_plane(grad_mine, partner) for partner in PARTNERS))

    there = input_part(other, grad_other, after(gate_weight, saved), branch_other)
    here = input_part(mine, grad_mine, gate_weight, branch_mine)
    total, *sends = combine(mine, here, to_other_core(there))
    terms = [to_chip(send, partner) for send, partner in zip(sends, PARTNERS)]

    gated = lax.all_gather(after(gated, there), "col", axis=0, tiled=True)
    in_weight_grad = in_grad(mine, branch, grad_mine, grad_other, after(saved, total))
    in_weight_grad, total = lax.optimization_barrier((in_weight_grad, total))
    out_weight_grad = out_grad(mine, gated, after(cot_mine, total), cot_other, rest)
    for term in terms:
        total = total + term.astype(F32)
    return (total.astype(BF16), scan_grad, in_weight_grad, out_weight_grad)


def gate_backward(summed, scan_output, gate_input):
    gate_value = gate_input.astype(jnp.float32)
    sigmoid_gate = jax.nn.sigmoid(gate_value)
    silu_gate = gate_value * sigmoid_gate
    scan_value = scan_output.astype(jnp.float32)
    gated = (scan_value * silu_gate).astype(jnp.bfloat16)
    gate_grad = (
        summed * scan_value * sigmoid_gate * (1.0 + gate_value * (1.0 - sigmoid_gate))
    ).astype(jnp.bfloat16)
    scan_grad = (summed * silu_gate).astype(jnp.bfloat16)
    return (gated, gate_grad, scan_grad)


def per_device(
    out_cotangent, saved_input, scan_output, gate_input, branch_grad, out_weight, in_weight
):
    cotangent = lax.all_gather(out_cotangent, "row", axis=0, tiled=True)
    shares = lax.psum_scatter(
        lax.dot_general(
            cotangent, out_weight, (((1,), (1,)), ((), ())), preferred_element_type=jnp.float32
        ).astype(jnp.bfloat16),
        "col",
        scatter_dimension=0,
        tiled=True,
    ).astype(jnp.float32)
    gated, gate_grad, scan_grad = gate_backward(shares, scan_output, gate_input)
    gated_all, branch_all, gate_grad_all = (
        lax.all_gather(gated, "col", axis=0, tiled=True),
        lax.all_gather(branch_grad, "col", axis=0, tiled=True),
        lax.all_gather(gate_grad, "col", axis=0, tiled=True),
    )
    out_weight_grad = lax.dot_general(
        gated_all, cotangent, (((0,), (0,)), ((), ())), preferred_element_type=jnp.float32
    )
    total = lax.dot_general(
        branch_all, in_weight[:, 0, :], (((1,), (1,)), ((), ())), preferred_element_type=jnp.float32
    ) + lax.dot_general(
        gate_grad_all, in_weight[:, 1, :], (((1,), (1,)), ((), ())), preferred_element_type=jnp.float32
    )
    input_grad = lax.psum_scatter(
        total.astype(jnp.bfloat16), "row", scatter_dimension=0, tiled=True
    )
    piece = lax.all_gather(saved_input, "row", axis=0, tiled=True)
    in_weight_grad = jnp.stack(
        [
            lax.dot_general(piece, grad, (((0,), (0,)), ((), ())), preferred_element_type=jnp.float32)
            for grad in (branch_all, gate_grad_all)
        ],
        axis=1,
    )
    return (input_grad, scan_grad, in_weight_grad, out_weight_grad)


def solution(mesh):
    rows, columns = mesh.shape["row"], mesh.shape["col"]
    body = plane_per_device if (rows, columns) == (8, 4) else per_device
    return jax.shard_map(
        body,
        mesh=mesh,
        in_specs=(
            P("row", "col"),
            P("row", "col"),
            P("col", "row"),
            P("col", "row"),
            P("col", "row"),
            P("row", "col"),
            P("col", None, "row"),
        ),
        out_specs=(P("row", "col"), P("col", "row"), P("col", None, "row"), P("row", "col")),
        check_vma=False,
    )
```
